256 devices in a mesh: tm: 32 (over x_lo, z, core), clip: 8 (over y, x_hi).
Axes of the slice: x: 4 (x_hi: 2, x_lo: 2; x = x_hi * 2 + x_lo), y: 4, z: 8, core: 2. Of those that a mesh axis runs over, the one named last changes fastest.
Arguments:
- frames_in: bfloat16 [768, 256, 1024], P(('clip', 'tm')), parts along dimension 0, may hold values from -6 to 6
- gain_time: float32 [1024], replicated, may hold values from 0.1 to 1.9
- gain_space: float32 [1024], replicated, may hold values from 0.1 to 1.9
- w_tqkv: bfloat16 [1024, 3072], P('tm'), may hold values from -1 to 1, as said below
- w_tout: bfloat16 [1024, 1024], P('tm'), may hold values from -0.1875 to 0.1875
- w_sqkv: bfloat16 [1024, 3072], replicated, may hold values from -1 to 1, as said below
- w_sout: bfloat16 [1024, 1024], replicated, may hold values from -0.1875 to 0.1875
Outputs:
- frames_out: bfloat16 [768, 256, 1024], P(('clip', 'tm')), parts along dimension 0
The draws below stay inside these ranges and needn't reach their ends.
There are 8 independent parts, one for each index of `clip`. The reference program is written for one: setup_inputs(seed, part) draws one part's arguments, and reference() takes and returns one part's arrays. A program takes and returns all parts, laid end to end along the dimension named above; an argument that names none is the same for every part. Nothing has to cross between parts.
Inputs may be any that keep to these rules, and one draw needn't show every extreme that they name: `w_tqkv`: projection weights. `w_sqkv`: projection weights.
All inputs are finite; a program needn't handle non-finite values.
Results may differ from the reference program's by a relative error of at most 0.0051.
Values may be sent and summed in bfloat16 or wider, within the bound.
A program may use at most 128 MiB of HBM per device.

```python
import jax
import jax.numpy as jnp
from jax import lax

D = 1024
HEADS = 16
HEAD = 64
P_SIZE = 256
FRAMES = 96


def qkv_matrix(key, query_scale):
    keys_split = jax.random.split(key, 3)
    base_mat = jax.random.normal(keys_split[0], (D, D), jnp.float32) * (query_scale / D ** 0.5)
    noise_mat = jax.random.normal(keys_split[1], (D, D), jnp.float32) * (query_scale / D ** 0.5)
    key_mat = noise_mat
    value_mat = jax.random.normal(keys_split[2], (D, D), jnp.float32) / D ** 0.5
    joined = jnp.concatenate([base_mat, key_mat, value_mat], axis=1)
    return jnp.clip(joined, -1.0, 1.0).astype(jnp.bfloat16)


def draw_w_tqkv(key, part):
    key = jax.random.fold_in(key, 21)
    return qkv_matrix(key, 1.0)


def draw_w_sqkv(key, part):
    key = jax.random.fold_in(key, 37)
    return qkv_matrix(key, 1.0)


def draw_frames_in(key, part):
    key = jax.random.fold_in(key, 53)
    keys_split = jax.random.split(key, 1)
    fresh = jax.random.normal(keys_split[0], (FRAMES, P_SIZE, D), jnp.float32)
    return jnp.clip(fresh, -6.0, 6.0).astype(jnp.bfloat16)


def steps_of(rng, shape, cuts, low, high):
    loudness = 1.0
    for position, blocks in cuts:
        steps = jax.random.uniform(jax.random.fold_in(jax.random.fold_in(rng, 6), position), (blocks,), jnp.float32, low / len(cuts), high / len(cuts))
        loudness = loudness * jnp.repeat(jnp.exp(steps), shape[position] // blocks).reshape((-1,) + (1,) * (len(shape) - 1 - position))
    return loudness


def centred(key, shape, scale, most, cuts=(), kind=jnp.bfloat16):
    values = scale * jax.random.normal(key, shape, jnp.float32)
    if cuts:
        values = values * steps_of(key, shape, cuts, -0.22, 0.18)
    return jnp.clip(values, -most, most).astype(kind)


def setup_inputs(seed: int = 0, part: int = 0) -> dict:
    arg_keys = jax.random.split(jax.random.key(seed), 8)
    part_splits = jax.random.split(jax.random.fold_in(arg_keys[7], part), 8)
    frames_in = draw_frames_in(jax.random.fold_in(jax.random.fold_in(arg_keys[7], part), 71), part)
    gain_time = jnp.clip(1.0 + 0.18 * jax.random.normal(arg_keys[1], (D,), jnp.float32), 0.1, 1.9)
    gain_space = jnp.clip(1.0 + 0.18 * jax.random.normal(arg_keys[2], (D,), jnp.float32), 0.1, 1.9)
    w_tqkv = draw_w_tqkv(jax.random.fold_in(arg_keys[7], 71), part)
    w_tout = centred(arg_keys[4], (D, D), D ** -0.5, 0.1875, ((0, 32),))
    w_sqkv = draw_w_sqkv(jax.random.fold_in(arg_keys[7], 71), part)
    w_sout = centred(arg_keys[6], (D, D), D ** -0.5, 0.1875)
    return dict(frames_in=frames_in, gain_time=gain_time, gain_space=gain_space, w_tqkv=w_tqkv, w_tout=w_tout, w_sqkv=w_sqkv, w_sout=w_sout)


def norm_tokens(token_rows, gain):
    values = token_rows.astype(jnp.float32)
    average = lax.optimization_barrier(jnp.mean(values, axis=-1, keepdims=True))
    spread = lax.optimization_barrier(jnp.mean((values - average) ** 2, axis=-1, keepdims=True))
    return ((values - average) * lax.rsqrt(spread + 1e-05) * gain).astype(jnp.bfloat16)

def widen(array_in):
    return lax.optimization_barrier(array_in).astype(jnp.float32)

def attend(queries, keys_all, values_all):
    scores = jnp.einsum('shd,thd->hst', widen(queries), widen(keys_all)) * 0.125
    weights = jax.nn.softmax(scores, axis=-1).astype(jnp.bfloat16)
    mixed = jnp.einsum('hst,thd->shd', widen(weights), widen(values_all))
    return mixed.astype(jnp.bfloat16)

def reference(frames_in, gain_time, gain_space, w_tqkv, w_tout, w_sqkv, w_sout):
    frame_count, patch_count, width = frames_in.shape
    token_rows = frames_in.reshape(frame_count * patch_count, width)
    normed_time = norm_tokens(token_rows, gain_time)
    normed_space = norm_tokens(token_rows, gain_space)
    time_qkv = jnp.dot(normed_time, w_tqkv, preferred_element_type=jnp.float32).astype(jnp.bfloat16)
    time_qkv = time_qkv.reshape(frame_count, patch_count, 3, HEADS, HEAD)
    by_patch = jnp.moveaxis(time_qkv, 1, 0)

    def time_block(block_in):
        return attend(block_in[:, 0], block_in[:, 1], block_in[:, 2])
    time_mixed = jnp.moveaxis(lax.map(time_block, by_patch), 0, 1).reshape(-1, width)
    time_branch = jnp.dot(time_mixed, w_tout, preferred_element_type=jnp.float32)
    space_qkv = jnp.dot(normed_space, w_sqkv, preferred_element_type=jnp.float32).astype(jnp.bfloat16)
    space_qkv = space_qkv.reshape(frame_count, patch_count, 3, HEADS, HEAD)

    def space_block(block_in):
        return attend(block_in[:, 0], block_in[:, 1], block_in[:, 2])
    space_mixed = lax.map(space_block, space_qkv).reshape(-1, width)
    space_branch = jnp.dot(space_mixed, w_sout, preferred_element_type=jnp.float32)
    result = token_rows.astype(jnp.float32) + time_branch + space_branch
    return result.astype(jnp.bfloat16).reshape(frame_count, patch_count, width)
```

```python
import functools
import math

import jax
import jax.numpy as jnp
from jax import lax
from jax.experimental import pallas as pl
from jax.experimental.pallas import tpu as pltpu
from jax.sharding import PartitionSpec as P

MESH = pl.DeviceIdType.MESH
D = 1024
FRAMES = 3
CHIPS = 16
BLOCK = 16
GROUPS = 4
PAIR = 128
EXP2_SCALE = 0.125 * math.log2(math.e)
F32 = jnp.float32
BF16 = jnp.bfloat16


def dot(a, b):
    return jnp.dot(a, b, preferred_element_type=F32)


def attend_pair(q, k, v):
    n = q.shape[0]
    low = lax.broadcasted_iota(jnp.int32, q.shape, 1) < PAIR // 2
    zero = jnp.zeros_like(q)
    stacked = jnp.concatenate([jnp.where(low, q, zero), jnp.where(low, zero, q)], axis=0).astype(BF16)
    s = lax.dot_general(stacked, k, (((1,), (1,)), ((), ())), preferred_element_type=F32)
    e = jnp.exp2((s - jnp.max(s, axis=-1, keepdims=True)) * EXP2_SCALE)
    p = (e * (1.0 / jnp.sum(e, axis=-1, keepdims=True))).astype(BF16)
    o = dot(p, v)
    return jnp.where(low, o[:n], o[n:])


def kernel(
    x_hbm, gt_ref, gs_ref, wt_hbm, wto_hbm, ws_hbm, wso_hbm, out_hbm,
    xv, nt, ns, tok, ws, wso, wst, cb, wt, wo, acc, mixs, qkvf, mixf, sb, eb, ret, ob,
    ld, sib, fsend, frecv, csend, crecv, zsend, zrecv, ysend, yrecv, losend, lorecv,
    hisend, hirecv, wsend, wrecv, wloc, esend, erecv, rsend, rrecv, outsem,
):
    tm = lax.axis_index("tm")
    cl = lax.axis_index("clip")
    core = tm % 2
    chip = tm // 2
    xl = chip // 8
    z = chip % 8
    y = cl // 2
    xh = cl % 2

    def chip_by(k, sign):
        dx = 1 - k % 2
        m = k // 2
        dz = 4 + (1 - 2 * (m % 2)) * ((m + 1) // 2)
        return (xl + dx - 2 * dx * xl) * 8 + (z + sign * dz + 8) % 8

    def remote(src, dst, s, r, to):
        return pltpu.make_async_remote_copy(
            src_ref=src, dst_ref=dst, send_sem=s, recv_sem=r, device_id=to, device_id_type=MESH
        )

    sibling = (chip * 2 + 1 - core, cl)
    lo_peer = (((1 - xl) * 8 + z) * 2 + core, cl)
    hi_peer = (((1 - xl) * 8 + z) * 2 + core, y * 2 + 1 - xh)

    def y_peer(d):
        return (tm, ((y + d) % 4) * 2 + xh)

    def cols(kind, half):
        return pl.ds(pl.multiple_of(kind * D + half * 512 + y * PAIR, PAIR), PAIR)

    load_x = pltpu.make_async_copy(x_hbm, xv, ld.at[0])
    load_w = []
    for t in range(4):
        src, kind = (wt_hbm, t) if t < 3 else (wto_hbm, 0)
        part = pl.ds(t * PAIR, PAIR)
        load_w.append(pltpu.make_async_copy(src.at[:, cols(kind, 1 - core)], wst.at[:, part], ld.at[1 + t]))
        load_w.append(pltpu.make_async_copy(src.at[:, cols(kind, core)], cb.at[core, :, part], ld.at[5 + t]))
    load_ws = pltpu.make_async_copy(ws_hbm, ws, ld.at[9])
    load_wso = pltpu.make_async_copy(wso_hbm, wso, ld.at[10])
    for c in load_w:
        c.start()
    load_x.start()
    load_ws.start()
    load_wso.start()

    barrier = pltpu.get_barrier_semaphore()

    def greet(k, carry):
        pl.semaphore_signal(barrier, inc=1, device_id=(chip_by(k, 1) * 2 + core, cl), device_id_type=MESH)
        return carry

    lax.fori_loop(0, CHIPS - 1, greet, 0)
    for to in (sibling, hi_peer, y_peer(1), y_peer(2), y_peer(3)):
        pl.semaphore_signal(barrier, inc=1, device_id=to, device_id_type=MESH)
    pl.semaphore_wait(barrier, CHIPS + 4)

    for c in load_w:
        c.wait()
    to_sib = remote(wst, cb.at[core], sib.at[0], sib.at[1], sibling)
    to_sib.start()

    gain_t = gt_ref[...]
    gain_s = gs_ref[...]

    def norm(target):
        for f in range(FRAMES):
            v = xv[f, target].astype(F32)
            c = v - jnp.mean(v, axis=-1, keepdims=True)
            n = c * lax.rsqrt(jnp.mean(c * c, axis=-1, keepdims=True) + 1e-5)
            nt[f, target] = (n * gain_t).astype(BF16)
            ns[f, target] = (n * gain_s).astype(BF16)

    load_x.wait()
    norm(chip)

    to_sib.wait_recv()

    def z_copy(d):
        to = ((xl * 8 + (z + d) % 8) * 2 + core, cl)
        return remote(cb, wt.at[y, chip], zsend.at[d - 1], zrecv.at[d - 1], to)

    def z_start(i, carry):
        z_copy(i).start()
        return carry

    lax.fori_loop(1, 8, z_start, 0)
    own_w = pltpu.make_async_copy(cb, wt.at[y, chip], wloc.at[4])
    own_w.start()

    def tok_copy(k):
        to = chip_by(k, 1)
        return remote(nt.at[:, to], tok.at[chip, core], fsend.at[k], frecv.at[k], (to * 2 + core, cl))

    def tok_start(k, carry):
        norm(chip_by(k, 1))
        tok_copy(k).start()
        return carry

    lax.fori_loop(0, CHIPS - 1, tok_start, 0)
    own_tok = pltpu.make_async_copy(nt.at[:, chip], tok.at[chip, core], wloc.at[5])
    own_tok.start()

    def share_copy(k, src):
        js = chip_by(k, -1)
        return remote(src, tok.at[js, core], csend.at[k], crecv.at[k], sibling)

    share_own = share_copy(CHIPS - 1, nt.at[:, chip])
    share_own.start()

    def space_frame(f):
        def quad(h, carry):
            a = ns[f].reshape(CHIPS * BLOCK, D)
            c0 = pl.multiple_of(h * 256, 256)
            q = dot(a, ws[:, pl.ds(c0, 256)])
            k = dot(a, ws[:, pl.ds(c0 + D, 256)]).astype(BF16)
            v = dot(a, ws[:, pl.ds(c0 + 2 * D, 256)]).astype(BF16)
            for i in range(2):
                part = slice(i * PAIR, (i + 1) * PAIR)
                o = attend_pair(q[:, part], k[:, part], v[:, part])
                mixs[:, pl.ds(pl.multiple_of(c0 + i * PAIR, PAIR), PAIR)] = o.astype(BF16)
            return carry

        lax.fori_loop(0, 4, quad, 0)

        def project(h, carry):
            c = pl.ds(pl.multiple_of(h * 256, 256), 256)
            xs = xv[f, :, :, c].reshape(CHIPS * BLOCK, 256).astype(F32)
            acc[f, :, c] = xs + dot(mixs[...], wso[:, c])
            return carry

        lax.fori_loop(0, 4, project, 0)

    def y_copy(d):
        part = wt.at[y, pl.ds(xl * 8, 8)]
        return remote(part, part, ysend.at[d - 1], yrecv.at[d - 1], y_peer(d))

    def x_copies(d):
        g = (y + 4 - d) % 4
        lo = wt.at[g, pl.ds(xl * 8, 3)]
        hi = wt.at[g, pl.ds(xl * 8 + 3, 5)]
        return (
            remote(lo, lo, losend.at[d], lorecv.at[d], lo_peer),
            remote(hi, hi, hisend.at[d], hirecv.at[d], hi_peer),
        )

    def x_start(d):
        for c in x_copies(d):
            c.start()

    load_ws.wait()
    load_wso.wait()
    space_frame(0)

    def z_wait(i, carry):
        z_copy(i).wait_recv()
        return carry

    lax.fori_loop(1, 8, z_wait, 0)
    own_w.wait()
    for d in (1, 3, 2):
        y_copy(d).start()
    x_start(0)
    space_frame(1)
    for d in (1, 3):
        y_copy(d).wait_recv()
        x_start(d)
    space_frame(2)
    y_copy(2).wait_recv()
    x_start(2)

    def tok_share(k, carry):
        tok_copy(k).wait_recv()
        share_copy(k, tok.at[chip_by(k, -1), core]).start()
        return carry

    lax.fori_loop(0, CHIPS - 1, tok_share, 0)
    own_tok.wait()

    for d in range(4):
        for c in x_copies(d):
            c.wait_recv()

    def wo_copies(g):
        src = wt.at[g, :, :, :, pl.ds(3 * PAIR, PAIR)]
        dst = wo.at[:, :, :, pl.ds(pl.multiple_of(core * 512 + g * PAIR, PAIR), PAIR)]
        return (
            pltpu.make_async_copy(src, dst, wloc.at[g]),
            remote(src, dst, wsend.at[g], wrecv.at[g], sibling),
        )

    for g in range(GROUPS):
        for c in wo_copies(g):
            c.start()

    def share_wait(k, carry):
        share_copy(k, tok.at[chip_by(k, -1), core]).wait_recv()
        return carry

    lax.fori_loop(0, CHIPS, share_wait, 0)

    def eb_copy(g):
        dst = sb.at[g, :, :, :, pl.ds(pl.multiple_of(core * PAIR, PAIR), PAIR)]
        return remote(eb.at[g], dst, esend.at[g], erecv.at[g], sibling)

    def ret_copy(g, k):
        to = chip_by(k, 1)
        return remote(sb.at[g, to], ret.at[g, :, chip], rsend.at[g, k], rrecv.at[g, k], (to * 2 + core, cl))

    def time_group(g, carry):
        def project(mb, carry):
            a = tok[pl.ds(mb * 4, 4)].reshape(384, D)
            w = wt[g, :, :, :, : 3 * PAIR].reshape(D, 3 * PAIR)
            qkv = dot(a, w)
            for t in range(3):
                qkvf[t, pl.ds(pl.multiple_of(mb * 384, 384), 384), :] = qkv[:, t * PAIR : (t + 1) * PAIR]
            return carry

        lax.fori_loop(0, 4, project, 0)

        def patches(i, carry):
            for u in range(4):
                rows = pl.ds(i * 4 + u, 96, stride=BLOCK)
                q = qkvf[0, rows, :]
                k = qkvf[1, rows, :].astype(BF16)
                v = qkvf[2, rows, :].astype(BF16)
                mixf[rows, :] = attend_pair(q, k, v)
            return carry

        lax.fori_loop(0, BLOCK // 4, patches, 0)

        def settle(j, carry):
            mine = pl.ds(pl.multiple_of(j * 96 + core * 48, 16), 48)
            other = pl.ds(pl.multiple_of(j * 96 + (1 - core) * 48, 16), 48)
            here = pl.ds(pl.multiple_of(core * PAIR, PAIR), PAIR)
            sb[g, j, :, :, here] = mixf[mine, :].astype(BF16).reshape(FRAMES, BLOCK, PAIR)
            eb[g, j] = mixf[other, :].astype(BF16).reshape(FRAMES, BLOCK, PAIR)
            return carry

        lax.fori_loop(0, CHIPS, settle, 0)
        eb_copy(g).start()
        eb_copy(g).wait_recv()

        def ret_start(k, carry):
            ret_copy(g, k).start()
            return carry

        lax.fori_loop(0, CHIPS - 1, ret_start, 0)
        ret[g, :, chip] = sb[g, chip]
        return carry

    lax.fori_loop(0, GROUPS, time_group, 0)

    for g in range(GROUPS):
        here, there = wo_copies(g)
        here.wait()
        there.wait_recv()

    def final(g, last):
        def ret_wait(k, carry):
            ret_copy(g, k).wait_recv()
            return carry

        lax.fori_loop(0, CHIPS - 1, ret_wait, 0)

        def project(f, carry):
            a = ret[g, f].reshape(CHIPS * BLOCK, 256)
            for h in range(2):
                c = pl.ds(h * 512, 512)
                w = jnp.concatenate(
                    [
                        wo[pl.ds(2 * g, 2), :, :, c].reshape(PAIR, 512),
                        wo[pl.ds(8 + 2 * g, 2), :, :, c].reshape(PAIR, 512),
                    ],
                    axis=0,
                )
                total = acc[f, :, c] + dot(a, w)
                if last:
                    ob[f, :, c] = total.astype(BF16)
                else:
                    acc[f, :, c] = total
            if last:
                pltpu.make_async_copy(ob.at[f], out_hbm.at[f], outsem.at[f]).start()
            return carry

        lax.fori_loop(0, FRAMES, project, 0)

    def final_step(g, carry):
        final(g, False)
        return carry

    lax.fori_loop(0, GROUPS - 1, final_step, 0)
    final(GROUPS - 1, True)

    to_sib.wait_send()

    def z_sent(i, carry):
        z_copy(i).wait_send()
        return carry

    lax.fori_loop(1, 8, z_sent, 0)
    for d in (1, 3, 2):
        y_copy(d).wait_send()
    for d in range(4):
        for c in x_copies(d):
            c.wait_send()
    for g in range(GROUPS):
        wo_copies(g)[1].wait_send()

    def tok_sent(k, carry):
        tok_copy(k).wait_send()
        return carry

    lax.fori_loop(0, CHIPS - 1, tok_sent, 0)

    def share_sent(k, carry):
        share_copy(k, tok.at[chip_by(k, -1), core]).wait_send()
        return carry

    lax.fori_loop(0, CHIPS, share_sent, 0)

    def ret_sent(i, carry):
        g = i // 15
        ret_copy(g, i % 15).wait_send()
        return carry

    lax.fori_loop(0, GROUPS * (CHIPS - 1), ret_sent, 0)

    def eb_sent(g, carry):
        eb_copy(g).wait_send()
        return carry

    lax.fori_loop(0, GROUPS, eb_sent, 0)
    for f in range(FRAMES):
        pltpu.make_async_copy(ob.at[f], out_hbm.at[f], outsem.at[f]).wait()


def body(frames_in, gain_time, gain_space, w_tqkv, w_tout, w_sqkv, w_sout):
    dma = pltpu.SemaphoreType.DMA
    vmem = pl.BlockSpec(memory_space=pltpu.VMEM)
    hbm = pl.BlockSpec(memory_space=pl.ANY)
    out = pl.pallas_call(
        kernel,
        out_shape=jax.ShapeDtypeStruct((FRAMES, CHIPS * BLOCK, D), BF16),
        in_specs=[hbm, vmem, vmem, hbm, hbm, hbm, hbm],
        out_specs=hbm,
        scratch_shapes=[
            pltpu.VMEM((FRAMES, CHIPS, BLOCK, D), BF16),
            pltpu.VMEM((FRAMES, CHIPS, BLOCK, D), BF16),
            pltpu.VMEM((FRAMES, CHIPS, BLOCK, D), BF16),
            pltpu.VMEM((CHIPS, 2, FRAMES, BLOCK, D), BF16),
            pltpu.VMEM((D, 3 * D), BF16),
            pltpu.VMEM((D, D), BF16),
            pltpu.VMEM((32, 512), BF16),
            pltpu.VMEM((2, 32, 512), BF16),
            pltpu.VMEM((GROUPS, CHIPS, 2, 32, 512), BF16),
            pltpu.VMEM((CHIPS, 2, 32, D), BF16),
            pltpu.VMEM((FRAMES, CHIPS * BLOCK, D), F32),
            pltpu.VMEM((CHIPS * BLOCK, D), BF16),
            pltpu.VMEM((3, CHIPS * 96, PAIR), F32),
            pltpu.VMEM((CHIPS * 96, PAIR), F32),
            pltpu.VMEM((GROUPS, CHIPS, FRAMES, BLOCK, 2 * PAIR), BF16),
            pltpu.VMEM((GROUPS, CHIPS, FRAMES, BLOCK, PAIR), BF16),
            pltpu.VMEM((GROUPS, FRAMES, CHIPS, BLOCK, 2 * PAIR), BF16),
            pltpu.VMEM((FRAMES, CHIPS * BLOCK, D), BF16),
            dma((11,)),
            dma((2,)),
            dma((15,)), dma((15,)),
            dma((16,)), dma((16,)),
            dma((7,)), dma((7,)),
            dma((3,)), dma((3,)),
            dma((4,)), dma((4,)),
            dma((4,)), dma((4,)),
            dma((4,)), dma((4,)),
            dma((6,)),
            dma((4,)), dma((4,)),
            dma((4, 15)), dma((4, 15)),
            dma((3,)),
        ],
        compiler_params=pltpu.CompilerParams(
            collective_id=0, has_side_effects=True, vmem_limit_bytes=56 * 2**20
        ),
        name="encoder_block",
    )(
        frames_in.reshape(FRAMES, CHIPS, BLOCK, D),
        gain_time.reshape(1, D),
        gain_space.reshape(1, D),
        w_tqkv, w_tout, w_sqkv, w_sout,
    )
    return out


def solution(mesh):
    in_specs = (P(("clip", "tm"), None, None), P(), P(), P("tm", None), P("tm", None), P(), P())
    out_specs = P(("clip", "tm"), None, None)
    return jax.shard_map(body, mesh=mesh, in_specs=in_specs, out_specs=out_specs, check_vma=False)
```

```python
import functools
import math

import jax
import jax.numpy as jnp
from jax import lax
from jax.experimental import pallas as pl
from jax.experimental.pallas import tpu as pltpu
from jax.sharding import PartitionSpec as P

MESH = pl.DeviceIdType.MESH
D = 1024
FRAMES = 3
CHIPS = 16
BLOCK = 16
GROUPS = 4
PAIR = 128
Z_ORDER = (1, 7, 2, 6, 3, 5, 4)
WINDOW = 14
IN_TILES = (pl.ds(0, 2), pl.ds(2, 1))
OUT_TILES = (pl.ds(0, 1), pl.ds(1, 2))
EXP2_SCALE = 0.125 * math.log2(math.e)
F32 = jnp.float32
BF16 = jnp.bfloat16


def dot(a, b):
    return jnp.dot(a, b, preferred_element_type=F32)


def attend_pairs(triples):
    n = triples[0][0].shape[0]
    low = lax.broadcasted_iota(jnp.int32, (n, PAIR), 1) < PAIR // 2
    both = jnp.concatenate([low, low], axis=1)
    zero = jnp.zeros((n, PAIR), F32)
    stacked = [
        jnp.concatenate([jnp.where(low, q, zero), jnp.where(low, zero, q)], axis=0).astype(BF16)
        for q, _, _ in triples
    ]
    scores = [
        lax.dot_general(q, k, (((1,), (1,)), ((), ())), preferred_element_type=F32)
        for q, (_, k, _) in zip(stacked, triples)
    ]
    tops = [jnp.max(s, axis=-1, keepdims=True) for s in scores]
    weights = [jnp.exp2((s - m) * EXP2_SCALE).astype(BF16) for s, m in zip(scores, tops)]
    mixed = [
        dot(e, jnp.concatenate([v, jnp.ones_like(v)], axis=1)) for e, (_, _, v) in zip(weights, triples)
    ]
    out = []
    for o in mixed:
        o = jnp.where(both, o[:n], o[n:])
        out.append(o[:, :PAIR] / o[:, PAIR:])
    return out


def kernel(
    x_hbm, gt_ref, gs_ref, wt_hbm, wto_hbm, ws_hbm, wso_hbm, out_hbm,
    xv, nt, ns, tok, ws, wso, wst, cb, wz, wt, wot, wo, acc, mixs, qa, qb, ma, mb, sb, eb, ret, ob,
    ld, sib, fsend, frecv, csend, crecv, zsend, zrecv, ysend, yrecv, losend, lorecv,
    hisend, hirecv, wsend, wrecv, wloc, esend, erecv, rsend, rrecv, outsem,
):
    tm = lax.axis_index("tm")
    cl = lax.axis_index("clip")
    core = tm % 2
    chip = tm // 2
    xl = chip // 8
    z = chip % 8
    y = cl // 2
    xh = cl % 2

    def chip_by(k, sign):
        last = k // 14
        dx = k % 2 + last - 2 * last * (k % 2)
        m = k // 2
        odd = m % 2
        dz = ((1 - odd) * (m // 2 + 1) + odd * (8 - (m + 1) // 2)) * (1 - last)
        return (xl + dx - 2 * dx * xl) * 8 + (z + sign * dz + 8) % 8

    def remote(src, dst, s, r, to):
        return pltpu.make_async_remote_copy(
            src_ref=src, dst_ref=dst, send_sem=s, recv_sem=r, device_id=to, device_id_type=MESH
        )

    sibling = (chip * 2 + 1 - core, cl)
    lo_peer = (((1 - xl) * 8 + z) * 2 + core, cl)
    hi_peer = (((1 - xl) * 8 + z) * 2 + core, y * 2 + 1 - xh)

    def y_peer(d):
        return (tm, ((y + d) % 4) * 2 + xh)

    def cols(kind, half):
        return pl.ds(pl.multiple_of(kind * D + half * 512 + y * PAIR, PAIR), PAIR)

    load_x = pltpu.make_async_copy(x_hbm, xv, ld.at[0])
    load_w = []
    for t in range(4):
        src, kind = (wt_hbm, t) if t < 3 else (wto_hbm, 0)
        part = pl.ds(t * PAIR, PAIR)
        load_w.append(pltpu.make_async_copy(src.at[:, cols(kind, 1 - core)], wst.at[:, part], ld.at[1 + t]))
        load_w.append(pltpu.make_async_copy(src.at[:, cols(kind, core)], cb.at[core, :, part], ld.at[5 + t]))
    load_ws = pltpu.make_async_copy(ws_hbm, ws, ld.at[9])
    load_wso = pltpu.make_async_copy(wso_hbm, wso, ld.at[10])
    load_x.start()
    for c in load_w:
        c.start()
    load_ws.start()
    load_wso.start()

    barrier = pltpu.get_barrier_semaphore()

    def greet(k, carry):
        pl.semaphore_signal(barrier, inc=1, device_id=(chip_by(k, 1) * 2 + core, cl), device_id_type=MESH)
        return carry

    lax.fori_loop(0, CHIPS - 1, greet, 0)
    for to in (sibling, hi_peer, y_peer(1), y_peer(2), y_peer(3)):
        pl.semaphore_signal(barrier, inc=1, device_id=to, device_id_type=MESH)

    gain_t = gt_ref[...]
    gain_s = gs_ref[...]
    load_x.wait()

    def norm(j, carry):
        normed = []
        for f in range(FRAMES):
            v = xv[f, j].astype(F32)
            c = v - jnp.mean(v, axis=-1, keepdims=True)
            n = c * lax.rsqrt(jnp.mean(c * c, axis=-1, keepdims=True) + 1e-5)
            normed.append(n * gain_t)
            ns[f, j] = (n * gain_s).astype(BF16)
        nt[j, 0] = jnp.concatenate([normed[0][:8], normed[1][:8]], axis=0).astype(BF16)
        nt[j, 1] = normed[2].astype(BF16)
        nt[j, 2] = jnp.concatenate([normed[0][8:], normed[1][8:]], axis=0).astype(BF16)
        return carry

    lax.fori_loop(0, CHIPS, norm, 0)
    for c in load_w:
        c.wait()
    pl.semaphore_wait(barrier, CHIPS + 4)

    to_sib = remote(wst, cb.at[core], sib.at[0], sib.at[1], sibling)
    to_sib.start()

    def tok_copy(h, k):
        to = chip_by(k, 1)
        return remote(
            nt.at[to, IN_TILES[h]], tok.at[chip, core, IN_TILES[h]],
            fsend.at[h, k], frecv.at[h, k], (to * 2 + core, cl),
        )

    def tok_start(n, carry):
        h = n // (CHIPS - 1)
        for v in range(2):

            @pl.when(h == v)
            def _():
                tok_copy(v, n - v * (CHIPS - 1)).start()

        return carry

    def tok_sent(n, carry):
        h = n // (CHIPS - 1)
        for v in range(2):

            @pl.when(h == v)
            def _():
                tok_copy(v, n - v * (CHIPS - 1)).wait_send()

        return carry

    def tok_share(h):
        def share(k, carry):
            tok_copy(h, k).wait_recv()
            share_copy(h, k, tok.at[chip_by(k, -1), core]).start()
            return carry

        return share

    def share_copy(h, k, src):
        return remote(
            src.at[IN_TILES[h]], tok.at[chip_by(k, -1), core, IN_TILES[h]],
            csend.at[h, k], crecv.at[h, k], sibling,
        )

    lax.fori_loop(0, 4, tok_start, 0)

    def z_copy(kind, d):
        part = (slice(None), slice(None), pl.ds(0, 3 * PAIR) if kind == 0 else pl.ds(3 * PAIR, PAIR))
        to = ((xl * 8 + (z + d) % 8) * 2 + core, cl)
        return remote(cb.at[part], wz.at[z].at[part], zsend.at[kind, d - 1], zrecv.at[kind, d - 1], to)

    def z_start(kind):
        for d in Z_ORDER:
            z_copy(kind, d).start()

    def z_wait(kind):
        for d in Z_ORDER:
            z_copy(kind, d).wait_recv()

    to_sib.wait_recv()
    z_start(0)
    own_w = pltpu.make_async_copy(cb, wz.at[z], wloc.at[4])
    own_w.start()
    lax.fori_loop(4, WINDOW, tok_start, 0)
    own_tok = pltpu.make_async_copy(nt.at[chip], tok.at[chip, core], wloc.at[5])
    own_tok.start()
    for h in range(2):
        share_copy(h, CHIPS - 1, nt.at[chip]).start()

    def own_part(kind, first, count):
        part = pl.ds(0, 3 * PAIR) if kind == 0 else pl.ds(3 * PAIR, PAIR)
        return wz.at[pl.ds(first, count), :, :, part]

    def held(kind, g, first, count):
        return (wt, wot)[kind].at[g, pl.ds(xl * 8 + first, count)]

    def y_copy(kind, d):
        return remote(
            own_part(kind, 0, 8), held(kind, y, 0, 8),
            ysend.at[kind, d - 1], yrecv.at[kind, d - 1], y_peer(d),
        )

    def x_copies(kind, d):
        g = (y + 4 - d) % 4
        out = []
        for first, count, s, r, to in ((0, 3, losend, lorecv, lo_peer), (3, 5, hisend, hirecv, hi_peer)):
            dst = held(kind, g, first, count)
            src = own_part(kind, first, count) if d == 0 else dst
            out.append(remote(src, dst, s.at[kind, d], r.at[kind, d], to))
        return out

    def x_start(kind, d):
        for c in x_copies(kind, d):
            c.start()

    def y_start(kind):
        for d in (1, 3, 2):
            y_copy(kind, d).start()
        x_start(kind, 0)

    def keep_own(kind):
        return pltpu.make_async_copy(own_part(kind, 0, 8), held(kind, y, 0, 8), wloc.at[6 + kind])

    load_ws.wait()
    load_wso.wait()

    def space(i, carry):
        f = i // 4
        c0 = pl.multiple_of((i % 4) * 256, 256)
        a = ns[f].reshape(CHIPS * BLOCK, D)
        q = dot(a, ws[:, pl.ds(c0, 256)])
        k = dot(a, ws[:, pl.ds(c0 + D, 256)]).astype(BF16)
        v = dot(a, ws[:, pl.ds(c0 + 2 * D, 256)]).astype(BF16)
        parts = [slice(u * PAIR, (u + 1) * PAIR) for u in range(2)]
        for u, o in enumerate(attend_pairs([(q[:, p], k[:, p], v[:, p]) for p in parts])):
            mixs[:, pl.ds(pl.multiple_of(c0 + u * PAIR, PAIR), PAIR)] = o.astype(BF16)

        @pl.when(i % 4 == 3)
        def _():
            def project(h, carry):
                c = pl.ds(pl.multiple_of(h * 256, 256), 256)
                xs = xv[f, :, :, c].reshape(CHIPS * BLOCK, 256).astype(F32)
                acc[f, :, :, :, c] = (xs + dot(mixs[...], wso[:, c])).reshape(CHIPS, 2, 8, 256)
                return carry

            lax.fori_loop(0, 4, project, 0)

        @pl.when(i == 0)
        def _():
            z_wait(0)
            own_w.wait()
            y_start(0)
            keep_own(0).start()

        for u in range(2):
            tok_sent(2 * i + u, 0)

            @pl.when(2 * i + u + WINDOW < 2 * (CHIPS - 1))
            def _():
                tok_start(2 * i + u + WINDOW, 0)

        @pl.when((i >= 2) & (i < 9))
        def _():
            for u in range(2):
                tok_share(0)(2 * i - 4 + u, 0)

        @pl.when(i == 4)
        def _():
            for d in (1, 3):
                y_copy(0, d).wait_recv()
                x_start(0, d)

        @pl.when(i == 7)
        def _():
            y_copy(0, 2).wait_recv()
            x_start(0, 2)

        return carry

    lax.fori_loop(0, 12, space, 0)

    def share_wait(h):
        def wait(k, carry):
            share_copy(h, k, tok.at[chip_by(k, -1), core]).wait_recv()
            return carry

        return wait

    z_start(1)
    tok_share(0)(CHIPS - 2, 0)
    own_tok.wait()
    keep_own(0).wait()
    for d in range(4):
        for c in x_copies(0, d):
            c.wait_recv()
    lax.fori_loop(0, CHIPS, share_wait(0), 0)

    def wo_copies(g):
        dst = wo.at[:, :, :, pl.ds(pl.multiple_of(core * 512 + g * PAIR, PAIR), PAIR)]
        return (
            pltpu.make_async_copy(wot.at[g], dst, wloc.at[g]),
            remote(wot.at[g], dst, wsend.at[g], wrecv.at[g], sibling),
        )

    def eb_copy(h, g):
        dst = sb.at[g, :, OUT_TILES[h], :, pl.ds(pl.multiple_of(core * PAIR, PAIR), PAIR)]
        return remote(eb.at[g, :, OUT_TILES[h]], dst, esend.at[h, g], erecv.at[h, g], sibling)

    def ret_copy(h, g, k):
        to = chip_by(k, 1)
        return remote(
            sb.at[g, to, OUT_TILES[h]], ret.at[g, chip, OUT_TILES[h]],
            rsend.at[h, g, k], rrecv.at[h, g, k], (to * 2 + core, cl),
        )

    def send_back(h, g):
        eb_copy(h, g).wait_recv()

        def ret_start(k, carry):
            ret_copy(h, g, k).start()
            return carry

        lax.fori_loop(0, CHIPS - 1, ret_start, 0)
        ret[g, chip, OUT_TILES[h]] = sb[g, chip, OUT_TILES[h]]

    def attend_patches(qkv, out):
        def patches(i, carry):
            rows = [pl.ds(i * 4 + u, 96, stride=8) for u in range(4)]
            triples = [(qkv(0, r), qkv(1, r).astype(BF16), qkv(2, r).astype(BF16)) for r in rows]
            for r, o in zip(rows, attend_pairs(triples)):
                out[r, :] = o
            return carry

        lax.fori_loop(0, 2, patches, 0)

    here = pl.ds(pl.multiple_of(core * PAIR, PAIR), PAIR)

    def first_group(g, carry):
        def project(n, carry):
            a = tok[pl.ds(n * 8, 8), :, 0:2].reshape(512, D)
            r = dot(a, wt[g].reshape(D, 3 * PAIR))
            for t in range(3):
                part = r[:, t * PAIR : (t + 1) * PAIR]
                for i in range(16):
                    at = pl.multiple_of((n * 16 + i) * 24, 8)
                    qa[t, pl.ds(at, 24), :] = part[i * 32 : i * 32 + 24]
                    qb[g * 3 + t, pl.ds(at, 8), :] = part[i * 32 + 24 : i * 32 + 32]
            return carry

        lax.fori_loop(0, 2, project, 0)

        @pl.when(g > 0)
        def _():
            send_back(0, g - 1)

        attend_patches(lambda t, rows: qa[t, rows, :], ma.at[g])

        def settle(j, carry):
            for mine in range(2):
                at = (j * 2 + (core if mine else 1 - core)) * 24
                tile = ma[g, pl.ds(pl.multiple_of(at, 8), 16), :].astype(BF16)
                if mine:
                    sb[g, j, 0, :, here] = tile
                else:
                    eb[g, j, 0] = tile
            return carry

        lax.fori_loop(0, CHIPS, settle, 0)
        eb_copy(0, g).start()

        @pl.when(g > 0)
        def _():
            lax.fori_loop((g - 1) * 5, g * 5, tok_share(1), 0)

        @pl.when(g == 1)
        def _():
            z_wait(1)
            y_start(1)
            keep_own(1).start()

        return carry

    lax.fori_loop(0, GROUPS, first_group, 0)
    lax.fori_loop(0, CHIPS, share_wait(1), 0)

    def second_group(g, carry):
        def project(n, carry):
            a = tok[pl.ds(n * 8, 8), :, 2].reshape(256, D)
            r = dot(a, wt[g].reshape(D, 3 * PAIR))
            for t in range(3):
                part = r[:, t * PAIR : (t + 1) * PAIR]
                for i in range(16):
                    at = pl.multiple_of((n * 16 + i) * 24 + 8, 8)
                    qb[g * 3 + t, pl.ds(at, 16), :] = part[i * 16 : i * 16 + 16]
            return carry

        lax.fori_loop(0, 2, project, 0)

        @pl.when(g == 0)
        def _():
            send_back(0, GROUPS - 1)

        @pl.when(g > 0)
        def _():
            send_back(1, g - 1)

        attend_patches(lambda t, rows: qb[g * 3 + t, rows, :], mb)

        def settle(j, carry):
            for mine in range(2):
                at = (j * 2 + (core if mine else 1 - core)) * 24
                first = ma[g, pl.ds(pl.multiple_of(at + 16, 8), 8), :]
                rest = mb[pl.ds(pl.multiple_of(at, 8), 24), :]
                one = jnp.concatenate([first, rest[:8]], axis=0).astype(BF16)
                two = rest[8:].astype(BF16)
                if mine:
                    sb[g, j, 1, :, here] = one
                    sb[g, j, 2, :, here] = two
                else:
                    eb[g, j, 1] = one
                    eb[g, j, 2] = two
            return carry

        lax.fori_loop(0, CHIPS, settle, 0)
        eb_copy(1, g).start()

        @pl.when(g == 0)
        def _():
            for d in (1, 3, 2):
                y_copy(1, d).wait_recv()
                x_start(1, d)

        @pl.when(g == 2)
        def _():
            for d in range(4):
                for c in x_copies(1, d):
                    c.wait_recv()
            keep_own(1).wait()
            for n in range(GROUPS):
                for c in wo_copies(n):
                    c.start()

        return carry

    lax.fori_loop(0, GROUPS, second_group, 0)
    send_back(1, GROUPS - 1)

    for g in range(GROUPS):
        here_copy, there_copy = wo_copies(g)
        here_copy.wait()
        there_copy.wait_recv()

    def out_copy(n):
        part = pl.ds(n * 4, 4)
        return pltpu.make_async_copy(ob.at[:, part], out_hbm.at[:, part], outsem.at[n])

    def final(g, last):
        def ret_wait(k, carry):
            ret_copy(0, g, k).wait_recv()
            ret_copy(1, g, k).wait_recv()
            return carry

        lax.fori_loop(0, CHIPS - 1, ret_wait, 0)

        def project(n, carry):
            js = pl.ds(n * 4, 4)
            a = ret[g, js].reshape(192, 256)
            for h in range(2):
                c = pl.ds(h * 512, 512)
                w = jnp.concatenate(
                    [
                        wo[pl.ds(2 * g, 2), :, :, c].reshape(PAIR, 512),
                        wo[pl.ds(8 + 2 * g, 2), :, :, c].reshape(PAIR, 512),
                    ],
                    axis=0,
                )
                r = dot(a, w).reshape(4, 6, 8, 512)
                for f, (one, two) in enumerate(((0, 4), (1, 5), (2, 3))):
                    first = acc[f, js, 0, :, c] + r[:, one]
                    second = acc[f, js, 1, :, c] + r[:, two]
                    if last:
                        ob[f, js, :, c] = jnp.concatenate([first, second], axis=1).astype(BF16)
                    else:
                        acc[f, js, 0, :, c] = first
                        acc[f, js, 1, :, c] = second
            if last:
                out_copy(n).start()
            return carry

        lax.fori_loop(0, 4, project, 0)

    def final_step(g, carry):
        final(g, False)
        return carry

    lax.fori_loop(0, GROUPS - 1, final_step, 0)
    final(GROUPS - 1, True)

    to_sib.wait_send()
    for kind in range(2):
        for d in Z_ORDER:
            z_copy(kind, d).wait_send()
        for d in (1, 3, 2):
            y_copy(kind, d).wait_send()
        for d in range(4):
            for c in x_copies(kind, d):
                c.wait_send()
    for g in range(GROUPS):
        wo_copies(g)[1].wait_send()

    lax.fori_loop(24, 2 * (CHIPS - 1), tok_sent, 0)

    def share_sent(k, carry):
        for h in range(2):
            share_copy(h, k, tok.at[chip_by(k, -1), core]).wait_send()
        return carry

    lax.fori_loop(0, CHIPS, share_sent, 0)

    def back_sent(g, carry):
        def ret_sent(k, carry):
            for h in range(2):
                ret_copy(h, g, k).wait_send()
            return carry

        lax.fori_loop(0, CHIPS - 1, ret_sent, 0)
        for h in range(2):
            eb_copy(h, g).wait_send()
        return carry

    lax.fori_loop(0, GROUPS, back_sent, 0)
    for n in range(4):
        out_copy(n).wait()


def body(frames_in, gain_time, gain_space, w_tqkv, w_tout, w_sqkv, w_sout):
    dma = pltpu.SemaphoreType.DMA
    vmem = pl.BlockSpec(memory_space=pltpu.VMEM)
    hbm = pl.BlockSpec(memory_space=pl.ANY)
    out = pl.pallas_call(
        kernel,
        out_shape=jax.ShapeDtypeStruct((FRAMES, CHIPS, BLOCK, D), BF16),
        in_specs=[hbm, vmem, vmem, hbm, hbm, hbm, hbm],
        out_specs=hbm,
        scratch_shapes=[
            pltpu.VMEM((FRAMES, CHIPS, BLOCK, D), BF16),
            pltpu.VMEM((CHIPS, FRAMES, BLOCK, D), BF16),
            pltpu.VMEM((FRAMES, CHIPS, BLOCK, D), BF16),
            pltpu.VMEM((CHIPS, 2, FRAMES, BLOCK, D), BF16),
            pltpu.VMEM((D, 3 * D), BF16),
            pltpu.VMEM((D, D), BF16),
            pltpu.VMEM((32, 512), BF16),
            pltpu.VMEM((2, 32, 512), BF16),
            pltpu.VMEM((8, 2, 32, 512), BF16),
            pltpu.VMEM((GROUPS, CHIPS, 2, 32, 3 * PAIR), BF16),
            pltpu.VMEM((GROUPS, CHIPS, 2, 32, PAIR), BF16),
            pltpu.VMEM((CHIPS, 2, 32, D), BF16),
            pltpu.VMEM((FRAMES, CHIPS, 2, 8, D), F32),
            pltpu.VMEM((CHIPS * BLOCK, D), BF16),
            pltpu.VMEM((3, CHIPS * 48, PAIR), F32),
            pltpu.VMEM((GROUPS * 3, CHIPS * 48, PAIR), F32),
            pltpu.VMEM((GROUPS, CHIPS * 48, PAIR), F32),
            pltpu.VMEM((CHIPS * 48, PAIR), F32),
            pltpu.VMEM((GROUPS, CHIPS, FRAMES, BLOCK, 2 * PAIR), BF16),
            pltpu.VMEM((GROUPS, CHIPS, FRAMES, BLOCK, PAIR), BF16),
            pltpu.VMEM((GROUPS, CHIPS, FRAMES, BLOCK, 2 * PAIR), BF16),
            pltpu.VMEM((FRAMES, CHIPS, BLOCK, D), BF16),
            dma((11,)),
            dma((2,)),
            dma((2, 15)), dma((2, 15)),
            dma((2, 16)), dma((2, 16)),
            dma((2, 7)), dma((2, 7)),
            dma((2, 3)), dma((2, 3)),
            dma((2, 4)), dma((2, 4)),
            dma((2, 4)), dma((2, 4)),
            dma((4,)), dma((4,)),
            dma((8,)),
            dma((2, 4)), dma((2, 4)),
            dma((2, 4, 15)), dma((2, 4, 15)),
            dma((4,)),
        ],
        compiler_params=pltpu.CompilerParams(
            collective_id=0, has_side_effects=True, vmem_limit_bytes=56 * 2**20
        ),
        name="encoder_block",
    )(
        frames_in.reshape(FRAMES, CHIPS, BLOCK, D),
        gain_time.reshape(1, D),
        gain_space.reshape(1, D),
        w_tqkv, w_tout, w_sqkv, w_sout,
    )
    return out.reshape(FRAMES, CHIPS * BLOCK, D)


def solution(mesh):
    in_specs = (P(("clip", "tm"), None, None), P(), P(), P("tm", None), P("tm", None), P(), P())
    out_specs = P(("clip", "tm"), None, None)
    return jax.shard_map(body, mesh=mesh, in_specs=in_specs, out_specs=out_specs, check_vma=False)
```

```python
import functools
import math

import jax
import jax.numpy as jnp
from jax import lax
from jax.experimental import pallas as pl
from jax.experimental.pallas import tpu as pltpu
from jax.sharding import PartitionSpec as P

MESH = pl.DeviceIdType.MESH
D = 1024
FRAMES = 3
CHIPS = 16
BLOCK = 16
GROUPS = 4
PAIR = 128
Z_ORDER = (1, 7, 2, 6, 3, 5, 4)
WINDOW = 14
IN_TILES = (pl.ds(0, 2), pl.ds(2, 1))
OUT_TILES = (pl.ds(0, 1), pl.ds(1, 2))
EXP2_SCALE = 0.125 * math.log2(math.e)
F32 = jnp.float32
BF16 = jnp.bfloat16


def dot(a, b):
    return jnp.dot(a, b, preferred_element_type=F32)


def attend_pairs(triples):
    n = triples[0][0].shape[0]
    low = lax.broadcasted_iota(jnp.int32, (n, PAIR), 1) < PAIR // 2
    both = jnp.concatenate([low, low], axis=1)
    zero = jnp.zeros((n, PAIR), F32)
    stacked = [
        jnp.concatenate([jnp.where(low, q, zero), jnp.where(low, zero, q)], axis=0).astype(BF16)
        for q, _, _ in triples
    ]
    scores = [
        lax.dot_general(q, k, (((1,), (1,)), ((), ())), preferred_element_type=F32)
        for q, (_, k, _) in zip(stacked, triples)
    ]
    tops = [jnp.max(s, axis=-1, keepdims=True) for s in scores]
    weights = [jnp.exp2((s - m) * EXP2_SCALE).astype(BF16) for s, m in zip(scores, tops)]
    mixed = [
        dot(e, jnp.concatenate([v, jnp.ones_like(v)], axis=1)) for e, (_, _, v) in zip(weights, triples)
    ]
    out = []
    for o in mixed:
        o = jnp.where(both, o[:n], o[n:])
        out.append(o[:, :PAIR] / o[:, PAIR:])
    return out


def kernel(
    x_hbm, gt_ref, gs_ref, wt_hbm, wto_hbm, ws_hbm, wso_hbm, out_hbm,
    xv, nt, ns, tok, ws, wso, wst, cb, wz, wt, wot, wo, acc, mixs, qa, qb, ma, mb, sb, eb, ret, ob,
    ld, sib, fsend, frecv, csend, crecv, zsend, zrecv, ysend, yrecv, losend, lorecv,
    hisend, hirecv, wsend, wrecv, wloc, esend, erecv, rsend, rrecv, outsem,
):
    tm = lax.axis_index("tm")
    cl = lax.axis_index("clip")
    core = tm % 2
    chip = tm // 2
    xl = chip // 8
    z = chip % 8
    y = cl // 2
    xh = cl % 2

    def chip_by(k, sign):
        last = k // 14
        dx = k % 2 + last - 2 * last * (k % 2)
        m = k // 2
        odd = m % 2
        dz = ((1 - odd) * (m // 2 + 1) + odd * (8 - (m + 1) // 2)) * (1 - last)
        return (xl + dx - 2 * dx * xl) * 8 + (z + sign * dz + 8) % 8

    def remote(src, dst, s, r, to):
        return pltpu.make_async_remote_copy(
            src_ref=src, dst_ref=dst, send_sem=s, recv_sem=r, device_id=to, device_id_type=MESH
        )

    sibling = (chip * 2 + 1 - core, cl)
    lo_peer = (((1 - xl) * 8 + z) * 2 + core, cl)
    hi_peer = (((1 - xl) * 8 + z) * 2 + core, y * 2 + 1 - xh)

    def y_peer(d):
        return (tm, ((y + d) % 4) * 2 + xh)

    def cols(kind, half):
        return pl.ds(pl.multiple_of(kind * D + half * 512 + y * PAIR, PAIR), PAIR)

    load_x = pltpu.make_async_copy(x_hbm, xv, ld.at[0])
    load_w = []
    for t in range(4):
        src, kind = (wt_hbm, t) if t < 3 else (wto_hbm, 0)
        part = pl.ds(t * PAIR, PAIR)
        load_w.append(pltpu.make_async_copy(src.at[:, cols(kind, 1 - core)], wst.at[:, part], ld.at[1 + t]))
        load_w.append(pltpu.make_async_copy(src.at[:, cols(kind, core)], cb.at[core, :, part], ld.at[5 + t]))
    load_ws = pltpu.make_async_copy(ws_hbm, ws, ld.at[9])
    load_wso = pltpu.make_async_copy(wso_hbm, wso, ld.at[10])
    load_x.start()
    for c in load_w:
        c.start()
    load_ws.start()
    load_wso.start()

    barrier = pltpu.get_barrier_semaphore()

    def greet(k, carry):
        pl.semaphore_signal(barrier, inc=1, device_id=(chip_by(k, 1) * 2 + core, cl), device_id_type=MESH)
        return carry

    lax.fori_loop(0, CHIPS - 1, greet, 0)
    for to in (sibling, hi_peer, y_peer(1), y_peer(2), y_peer(3)):
        pl.semaphore_signal(barrier, inc=1, device_id=to, device_id_type=MESH)

    gain_t = gt_ref[...]
    gain_s = gs_ref[...]
    load_x.wait()

    def norm(j, carry):
        normed = []
        for f in range(FRAMES):
            v = xv[f, j].astype(F32)
            c = v - jnp.mean(v, axis=-1, keepdims=True)
            n = c * lax.rsqrt(jnp.mean(c * c, axis=-1, keepdims=True) + 1e-5)
            normed.append(n * gain_t)
            ns[f, j] = (n * gain_s).astype(BF16)
        nt[j, 0] = jnp.concatenate([normed[0][:8], normed[1][:8]], axis=0).astype(BF16)
        nt[j, 1] = normed[2].astype(BF16)
        nt[j, 2] = jnp.concatenate([normed[0][8:], normed[1][8:]], axis=0).astype(BF16)
        return carry

    lax.fori_loop(0, CHIPS, norm, 0)
    for c in load_w:
        c.wait()
    pl.semaphore_wait(barrier, CHIPS + 4)

    to_sib = remote(wst, cb.at[core], sib.at[0], sib.at[1], sibling)
    to_sib.start()

    def tok_copy(h, k):
        to = chip_by(k, 1)
        return remote(
            nt.at[to, IN_TILES[h]], tok.at[chip, core, IN_TILES[h]],
            fsend.at[h, k], frecv.at[h, k], (to * 2 + core, cl),
        )

    def tok_start(n, carry):
        h = n // (CHIPS - 1)
        for v in range(2):

            @pl.when(h == v)
            def _():
                tok_copy(v, n - v * (CHIPS - 1)).start()

        return carry

    def tok_sent(n, carry):
        h = n // (CHIPS - 1)
        for v in range(2):

            @pl.when(h == v)
            def _():
                tok_copy(v, n - v * (CHIPS - 1)).wait_send()

        return carry

    def tok_share(h):
        def share(k, carry):
            tok_copy(h, k).wait_recv()
            share_copy(h, k, tok.at[chip_by(k, -1), core]).start()
            return carry

        return share

    def share_copy(h, k, src):
        return remote(
            src.at[IN_TILES[h]], tok.at[chip_by(k, -1), core, IN_TILES[h]],
            csend.at[h, k], crecv.at[h, k], sibling,
        )

    lax.fori_loop(0, 4, tok_start, 0)

    def z_copy(kind, d):
        part = (slice(None), slice(None), pl.ds(0, 3 * PAIR) if kind == 0 else pl.ds(3 * PAIR, PAIR))
        to = ((xl * 8 + (z + d) % 8) * 2 + core, cl)
        return remote(cb.at[part], wz.at[z].at[part], zsend.at[kind, d - 1], zrecv.at[kind, d - 1], to)

    def z_start(kind):
        for d in Z_ORDER:
            z_copy(kind, d).start()

    def z_wait(kind):
        for d in Z_ORDER:
            z_copy(kind, d).wait_recv()

    to_sib.wait_recv()
    z_start(0)
    own_w = pltpu.make_async_copy(cb, wz.at[z], wloc.at[4])
    own_w.start()
    lax.fori_loop(4, WINDOW, tok_start, 0)
    own_tok = pltpu.make_async_copy(nt.at[chip], tok.at[chip, core], wloc.at[5])
    own_tok.start()
    for h in range(2):
        share_copy(h, CHIPS - 1, nt.at[chip]).start()

    def own_part(kind, first, count):
        part = pl.ds(0, 3 * PAIR) if kind == 0 else pl.ds(3 * PAIR, PAIR)
        return wz.at[pl.ds(first, count), :, :, part]

    def held(kind, g, first, count):
        return (wt, wot)[kind].at[g, pl.ds(xl * 8 + first, count)]

    def y_copy(kind, d):
        return remote(
            own_part(kind, 0, 8), held(kind, y, 0, 8),
            ysend.at[kind, d - 1], yrecv.at[kind, d - 1], y_peer(d),
        )

    def x_copies(kind, d):
        g = (y + 4 - d) % 4
        out = []
        for first, count, s, r, to in ((0, 3, losend, lorecv, lo_peer), (3, 5, hisend, hirecv, hi_peer)):
            dst = held(kind, g, first, count)
            src = own_part(kind, first, count) if d == 0 else dst
            out.append(remote(src, dst, s.at[kind, d], r.at[kind, d], to))
        return out

    def x_start(kind, d):
        for c in x_copies(kind, d):
            c.start()

    def y_start(kind):
        for d in (1, 3, 2):
            y_copy(kind, d).start()
        x_start(kind, 0)

    def keep_own(kind):
        return pltpu.make_async_copy(own_part(kind, 0, 8), held(kind, y, 0, 8), wloc.at[6 + kind])

    load_ws.wait()
    load_wso.wait()

    def space(i, carry):
        f = i // 4
        c0 = pl.multiple_of((i % 4) * 256, 256)
        a = ns[f].reshape(CHIPS * BLOCK, D)
        q = dot(a, ws[:, pl.ds(c0, 256)])
        k = dot(a, ws[:, pl.ds(c0 + D, 256)]).astype(BF16)
        v = dot(a, ws[:, pl.ds(c0 + 2 * D, 256)]).astype(BF16)
        parts = [slice(u * PAIR, (u + 1) * PAIR) for u in range(2)]
        for u, o in enumerate(attend_pairs([(q[:, p], k[:, p], v[:, p]) for p in parts])):
            mixs[:, pl.ds(pl.multiple_of(c0 + u * PAIR, PAIR), PAIR)] = o.astype(BF16)

        @pl.when(i % 4 == 3)
        def _():
            def project(h, carry):
                c = pl.ds(pl.multiple_of(h * 256, 256), 256)
                xs = xv[f, :, :, c].reshape(CHIPS * BLOCK, 256).astype(F32)
                acc[f, :, :, :, c] = (xs + dot(mixs[...], wso[:, c])).reshape(CHIPS, 2, 8, 256)
                return carry

            lax.fori_loop(0, 4, project, 0)

        @pl.when(i == 0)
        def _():
            z_wait(0)
            own_w.wait()
            y_start(0)
            keep_own(0).start()

        for u in range(2):
            tok_sent(2 * i + u, 0)

            @pl.when(2 * i + u + WINDOW < 2 * (CHIPS - 1))
            def _():
                tok_start(2 * i + u + WINDOW, 0)

        @pl.when((i >= 2) & (i < 9))
        def _():
            for u in range(2):
                tok_share(0)(2 * i - 4 + u, 0)

        @pl.when(i == 4)
        def _():
            for d in (1, 3):
                y_copy(0, d).wait_recv()
                x_start(0, d)

        @pl.when(i == 7)
        def _():
            y_copy(0, 2).wait_recv()
            x_start(0, 2)

        return carry

    lax.fori_loop(0, 12, space, 0)

    def share_wait(h):
        def wait(k, carry):
            share_copy(h, k, tok.at[chip_by(k, -1), core]).wait_recv()
            return carry

        return wait

    z_start(1)
    tok_share(0)(CHIPS - 2, 0)
    own_tok.wait()
    keep_own(0).wait()
    for d in range(4):
        for c in x_copies(0, d):
            c.wait_recv()
    lax.fori_loop(0, CHIPS, share_wait(0), 0)

    def wo_copies(g):
        dst = wo.at[:, :, :, pl.ds(pl.multiple_of(core * 512 + g * PAIR, PAIR), PAIR)]
        return (
            pltpu.make_async_copy(wot.at[g], dst, wloc.at[g]),
            remote(wot.at[g], dst, wsend.at[g], wrecv.at[g], sibling),
        )

    def eb_copy(h, g):
        dst = sb.at[g, :, OUT_TILES[h], :, pl.ds(pl.multiple_of(core * PAIR, PAIR), PAIR)]
        return remote(eb.at[g, :, OUT_TILES[h]], dst, esend.at[h, g], erecv.at[h, g], sibling)

    def ret_copy(h, g, k):
        to = chip_by(k, 1)
        return remote(
            sb.at[g, to, OUT_TILES[h]], ret.at[g, chip, OUT_TILES[h]],
            rsend.at[h, g, k], rrecv.at[h, g, k], (to * 2 + core, cl),
        )

    def send_back(h, g):
        eb_copy(h, g).wait_recv()

        def ret_start(k, carry):
            ret_copy(h, g, k).start()
            return carry

        lax.fori_loop(0, CHIPS - 1, ret_start, 0)
        ret[g, chip, OUT_TILES[h]] = sb[g, chip, OUT_TILES[h]]

    def attend_patches(qkv, out):
        def patches(i, carry):
            rows = [pl.ds(i * 8 + u, 96, stride=8) for u in range(8)]
            triples = [(qkv(0, r), qkv(1, r).astype(BF16), qkv(2, r).astype(BF16)) for r in rows]
            for r, o in zip(rows, attend_pairs(triples)):
                out[r, :] = o
            return carry

        patches(0, 0)

    here = pl.ds(pl.multiple_of(core * PAIR, PAIR), PAIR)

    def first_group(g, carry):
        def project(n, carry):
            a = tok[pl.ds(n * 8, 8), :, 0:2].reshape(512, D)
            r = dot(a, wt[g].reshape(D, 3 * PAIR))
            for t in range(3):
                part = r[:, t * PAIR : (t + 1) * PAIR]
                for i in range(16):
                    at = pl.multiple_of((n * 16 + i) * 24, 8)
                    qa[t, pl.ds(at, 24), :] = part[i * 32 : i * 32 + 24]
                    qb[g * 3 + t, pl.ds(at, 8), :] = part[i * 32 + 24 : i * 32 + 32]
            return carry

        lax.fori_loop(0, 2, project, 0)

        @pl.when(g > 0)
        def _():
            send_back(0, g - 1)

        attend_patches(lambda t, rows: qa[t, rows, :], ma.at[g])

        def settle(j, carry):
            for mine in range(2):
                at = (j * 2 + (core if mine else 1 - core)) * 24
                tile = ma[g, pl.ds(pl.multiple_of(at, 8), 16), :].astype(BF16)
                if mine:
                    sb[g, j, 0, :, here] = tile
                else:
                    eb[g, j, 0] = tile
            return carry

        lax.fori_loop(0, CHIPS, settle, 0)
        eb_copy(0, g).start()

        @pl.when(g > 0)
        def _():
            lax.fori_loop((g - 1) * 5, g * 5, tok_share(1), 0)

        @pl.when(g == 1)
        def _():
            z_wait(1)
            y_start(1)
            keep_own(1).start()

        return carry

    lax.fori_loop(0, GROUPS, first_group, 0)
    lax.fori_loop(0, CHIPS, share_wait(1), 0)

    def second_group(g, carry):
        def project():
            a = tok[:, :, 2].reshape(512, D)
            r = dot(a, wt[g].reshape(D, 3 * PAIR))
            for t in range(3):
                part = r[:, t * PAIR : (t + 1) * PAIR]
                for i in range(32):
                    at = i * 24 + 8
                    qb[g * 3 + t, pl.ds(at, 16), :] = part[i * 16 : i * 16 + 16]

        project()

        @pl.when(g == 0)
        def _():
            send_back(0, GROUPS - 1)

        @pl.when(g > 0)
        def _():
            send_back(1, g - 1)

        attend_patches(lambda t, rows: qb[g * 3 + t, rows, :], mb)

        def settle(j, carry):
            for mine in range(2):
                at = (j * 2 + (core if mine else 1 - core)) * 24
                first = ma[g, pl.ds(pl.multiple_of(at + 16, 8), 8), :]
                rest = mb[pl.ds(pl.multiple_of(at, 8), 24), :]
                one = jnp.concatenate([first, rest[:8]], axis=0).astype(BF16)
                two = rest[8:].astype(BF16)
                if mine:
                    sb[g, j, 1, :, here] = one
                    sb[g, j, 2, :, here] = two
                else:
                    eb[g, j, 1] = one
                    eb[g, j, 2] = two
            return carry

        lax.fori_loop(0, CHIPS, settle, 0)
        eb_copy(1, g).start()

        @pl.when(g == 0)
        def _():
            for d in (1, 3, 2):
                y_copy(1, d).wait_recv()
                x_start(1, d)

        @pl.when(g == 2)
        def _():
            for d in range(4):
                for c in x_copies(1, d):
                    c.wait_recv()
            keep_own(1).wait()
            for n in range(GROUPS):
                for c in wo_copies(n):
                    c.start()

        return carry

    lax.fori_loop(0, GROUPS, second_group, 0)
    send_back(1, GROUPS - 1)

    for g in range(GROUPS):
        here_copy, there_copy = wo_copies(g)
        here_copy.wait()
        there_copy.wait_recv()

    def out_copy(n):
        part = pl.ds(n * 4, 4)
        return pltpu.make_async_copy(ob.at[:, part], out_hbm.at[:, part], outsem.at[n])

    def final(g, last):
        def ret_wait(k, carry):
            ret_copy(0, g, k).wait_recv()
            ret_copy(1, g, k).wait_recv()
            return carry

        lax.fori_loop(0, CHIPS - 1, ret_wait, 0)

        def project(n, carry):
            js = pl.ds(n * 4, 4)
            a = ret[g, js].reshape(192, 256)
            for h in range(2):
                c = pl.ds(h * 512, 512)
                w = jnp.concatenate(
                    [
                        wo[pl.ds(2 * g, 2), :, :, c].reshape(PAIR, 512),
                        wo[pl.ds(8 + 2 * g, 2), :, :, c].reshape(PAIR, 512),
                    ],
                    axis=0,
                )
                r = dot(a, w).reshape(4, 6, 8, 512)
                for f, (one, two) in enumerate(((0, 4), (1, 5), (2, 3))):
                    first = acc[f, js, 0, :, c] + r[:, one]
                    second = acc[f, js, 1, :, c] + r[:, two]
                    if last:
                        ob[f, js, :, c] = jnp.concatenate([first, second], axis=1).astype(BF16)
                    else:
                        acc[f, js, 0, :, c] = first
                        acc[f, js, 1, :, c] = second
            if last:
                out_copy(n).start()
            return carry

        lax.fori_loop(0, 4, project, 0)

    def final_step(g, carry):
        final(g, False)
        return carry

    lax.fori_loop(0, GROUPS - 1, final_step, 0)
    final(GROUPS - 1, True)

    to_sib.wait_send()
    for kind in range(2):
        for d in Z_ORDER:
            z_copy(kind, d).wait_send()
        for d in (1, 3, 2):
            y_copy(kind, d).wait_send()
        for d in range(4):
            for c in x_copies(kind, d):
                c.wait_send()
    for g in range(GROUPS):
        wo_copies(g)[1].wait_send()

    lax.fori_loop(24, 2 * (CHIPS - 1), tok_sent, 0)

    def share_sent(k, carry):
        for h in range(2):
            share_copy(h, k, tok.at[chip_by(k, -1), core]).wait_send()
        return carry

    lax.fori_loop(0, CHIPS, share_sent, 0)

    def back_sent(g, carry):
        def ret_sent(k, carry):
            for h in range(2):
                ret_copy(h, g, k).wait_send()
            return carry

        lax.fori_loop(0, CHIPS - 1, ret_sent, 0)
        for h in range(2):
            eb_copy(h, g).wait_send()
        return carry

    lax.fori_loop(0, GROUPS, back_sent, 0)
    for n in range(4):
        out_copy(n).wait()


def body(frames_in, gain_time, gain_space, w_tqkv, w_tout, w_sqkv, w_sout):
    dma = pltpu.SemaphoreType.DMA
    vmem = pl.BlockSpec(memory_space=pltpu.VMEM)
    hbm = pl.BlockSpec(memory_space=pl.ANY)
    out = pl.pallas_call(
        kernel,
        out_shape=jax.ShapeDtypeStruct((FRAMES, CHIPS, BLOCK, D), BF16),
        in_specs=[hbm, vmem, vmem, hbm, hbm, hbm, hbm],
        out_specs=hbm,
        scratch_shapes=[
            pltpu.VMEM((FRAMES, CHIPS, BLOCK, D), BF16),
            pltpu.VMEM((CHIPS, FRAMES, BLOCK, D), BF16),
            pltpu.VMEM((FRAMES, CHIPS, BLOCK, D), BF16),
            pltpu.VMEM((CHIPS, 2, FRAMES, BLOCK, D), BF16),
            pltpu.VMEM((D, 3 * D), BF16),
            pltpu.VMEM((D, D), BF16),
            pltpu.VMEM((32, 512), BF16),
            pltpu.VMEM((2, 32, 512), BF16),
            pltpu.VMEM((8, 2, 32, 512), BF16),
            pltpu.VMEM((GROUPS, CHIPS, 2, 32, 3 * PAIR), BF16),
            pltpu.VMEM((GROUPS, CHIPS, 2, 32, PAIR), BF16),
            pltpu.VMEM((CHIPS, 2, 32, D), BF16),
            pltpu.VMEM((FRAMES, CHIPS, 2, 8, D), F32),
            pltpu.VMEM((CHIPS * BLOCK, D), BF16),
            pltpu.VMEM((3, CHIPS * 48, PAIR), F32),
            pltpu.VMEM((GROUPS * 3, CHIPS * 48, PAIR), F32),
            pltpu.VMEM((GROUPS, CHIPS * 48, PAIR), F32),
            pltpu.VMEM((CHIPS * 48, PAIR), F32),
            pltpu.VMEM((GROUPS, CHIPS, FRAMES, BLOCK, 2 * PAIR), BF16),
            pltpu.VMEM((GROUPS, CHIPS, FRAMES, BLOCK, PAIR), BF16),
            pltpu.VMEM((GROUPS, CHIPS, FRAMES, BLOCK, 2 * PAIR), BF16),
            pltpu.VMEM((FRAMES, CHIPS, BLOCK, D), BF16),
            dma((11,)),
            dma((2,)),
            dma((2, 15)), dma((2, 15)),
            dma((2, 16)), dma((2, 16)),
            dma((2, 7)), dma((2, 7)),
            dma((2, 3)), dma((2, 3)),
            dma((2, 4)), dma((2, 4)),
            dma((2, 4)), dma((2, 4)),
            dma((4,)), dma((4,)),
            dma((8,)),
            dma((2, 4)), dma((2, 4)),
            dma((2, 4, 15)), dma((2, 4, 15)),
            dma((4,)),
        ],
        compiler_params=pltpu.CompilerParams(
            collective_id=0, has_side_effects=True, vmem_limit_bytes=56 * 2**20
        ),
        name="encoder_block",
    )(
        frames_in.reshape(FRAMES, CHIPS, BLOCK, D),
        gain_time.reshape(1, D),
        gain_space.reshape(1, D),
        w_tqkv, w_tout, w_sqkv, w_sout,
    )
    return out.reshape(FRAMES, CHIPS * BLOCK, D)


def solution(mesh):
    in_specs = (P(("clip", "tm"), None, None), P(), P(), P("tm", None), P("tm", None), P(), P())
    out_specs = P(("clip", "tm"), None, None)
    return jax.shard_map(body, mesh=mesh, in_specs=in_specs, out_specs=out_specs, check_vma=False)
```
